512 devices in a mesh: row: 32 (over z, core), col: 16 (over x, y).
Axes of the slice: x: 4, y: 4, z: 16, core: 2. Of those that a mesh axis runs over, the one named last changes fastest.
Arguments:
- inputs: bfloat16 [384, 14848], P('row', 'col'), may hold values from -6 to 6
- out_grad: bfloat16 [384, 14848], P('col', 'row'), may hold values from -6 to 6
- w_up: bfloat16 [14848, 14848], P('col', 'row'), may hold values from -0.046875 to 0.046875
- w_down: bfloat16 [14848, 14848], P('col', 'row'), may hold values from -0.046875 to 0.046875
Outputs:
- input_grad: bfloat16 [384, 14848], P('row', 'col')
- up_grad: float32 [14848, 14848], P('col', 'row')
- down_grad: float32 [14848, 14848], P('col', 'row')
The draws below stay inside these ranges and needn't reach their ends.
All inputs are finite; a program needn't handle non-finite values.
Results may differ from the reference program's by a relative error of at most 0.0049.
Values may be sent and summed in bfloat16 or wider, within the bound.
A program may use at most 64 MiB of HBM per device.

```python
import math
import jax
import jax.numpy as jnp
from jax import lax

D = 14848
F = 14848
TOKENS = 384


def steps_of(key, extent, split, smallest, largest):
    gain = 1.0
    for axis_at, shards_of in split:
        steps = jax.random.uniform(jax.random.fold_in(jax.random.fold_in(key, 6), axis_at), (shards_of,), jnp.float32, smallest / len(split), largest / len(split))
        gain = gain * jnp.repeat(jnp.exp(steps), extent[axis_at] // shards_of).reshape((-1,) + (1,) * (len(extent) - 1 - axis_at))
    return gain


def scatter_about(own_key, extent, deviation, limit, cuts=(), dtype=jnp.bfloat16):
    loudness = steps_of(own_key, extent, cuts, -0.22, 0.18) if cuts else 1.0
    array = jax.random.normal(own_key, extent, jnp.float32) * deviation * loudness
    return jnp.minimum(jnp.maximum(array, -limit), limit).astype(dtype)


def setup_inputs(seed: int = 0) -> dict:
    seeds = jax.random.split(jax.random.key(seed), 5)
    inputs = scatter_about(seeds[0], (TOKENS, D), 1.0, 6.0, ((0, 32), (1, 16)))
    out_grad = scatter_about(seeds[1], (TOKENS, D), 1.0, 6.0, ((0, 16), (1, 32)))
    w_up = scatter_about(seeds[2], (D, F), D ** -0.5, 0.046875, ((0, 16), (1, 32)))
    w_down = scatter_about(seeds[3], (F, D), F ** -0.5, 0.046875, ((0, 16), (1, 32)))
    return {"inputs": inputs, "out_grad": out_grad, "w_up": w_up, "w_down": w_down}


def gelu_parts(hidden):
    cdf = 0.5 * (1.0 + jax.scipy.special.erf(hidden / math.sqrt(2.0)))
    pdf = jnp.exp(-0.5 * hidden * hidden) / math.sqrt(2.0 * math.pi)
    return (cdf, pdf)

def reference(inputs, out_grad, w_up, w_down):
    hidden = jnp.dot(inputs, w_up, preferred_element_type=jnp.float32)
    cdf, pdf = gelu_parts(hidden)
    activation = (hidden * cdf).astype(jnp.bfloat16)
    slope = cdf + hidden * pdf
    act_grad = lax.dot_general(out_grad, w_down, (((1,), (1,)), ((), ())), preferred_element_type=jnp.float32)
    hidden_grad = (act_grad * slope).astype(jnp.bfloat16)
    down_grad = lax.dot_general(activation, out_grad, (((0,), (0,)), ((), ())), preferred_element_type=jnp.float32)
    up_grad = lax.dot_general(inputs, hidden_grad, (((0,), (0,)), ((), ())), preferred_element_type=jnp.float32)
    input_grad = lax.dot_general(hidden_grad, w_up, (((1,), (1,)), ((), ())), preferred_element_type=jnp.float32).astype(jnp.bfloat16)
    return (input_grad, up_grad, down_grad)
```

```python
import math

import jax
import jax.numpy as jnp
from jax import lax
from jax.experimental import pallas as pl
from jax.experimental.pallas import tpu as pltpu
from jax.sharding import PartitionSpec as P

MESH = pl.DeviceIdType.MESH
BF16 = jnp.bfloat16
F32 = jnp.float32

NZ = 16
NP = 16
TB = 24
TD = 12
TOKENS = 384
W = 464
D2 = 928
COPIES = 240

PLANE = sorted(
    [(a, b) for a in range(4) for b in range(4) if (a, b) != (0, 0)],
    key=lambda o: -(min(o[0], 4 - o[0]) + min(o[1], 4 - o[1])),
)
FAR_FIRST = (2, 1, 3, 0)


def dot(a, b):
    return jnp.dot(a, b, preferred_element_type=F32)


def dot_nt(a, b):
    return lax.dot_general(a, b, (((1,), (1,)), ((), ())), preferred_element_type=F32)


def dot_tn(a, b):
    return lax.dot_general(a, b, (((0,), (0,)), ((), ())), preferred_element_type=F32)


def dense(blocks):
    n, t, w = blocks.shape
    return blocks.astype(F32).reshape(n * t, w).astype(BF16)


def gelu_parts(hidden):
    cdf = 0.5 * (1.0 + lax.erf(hidden / math.sqrt(2.0)))
    pdf = jnp.exp(-0.5 * hidden * hidden) / math.sqrt(2.0 * math.pi)
    return (cdf, pdf)


def unpad(which):
    i = lax.broadcasted_iota(jnp.int32, (4 * TB, 4 * 16), 0)
    j = lax.broadcasted_iota(jnp.int32, (4 * TB, 4 * 16), 1)
    hit = jnp.zeros((4 * TB, 4 * 16), F32)
    for a in range(4):
        low = TB * a + TD * which
        here = (i >= low) & (i < low + TD) & (j == i - low + 16 * a)
        hit = hit + jnp.where(here, 1.0, 0.0)
    return hit.astype(BF16)


def kernel(
    x_ref, dy_ref, wu_hbm, wd_hbm,
    xd_o, dyd_o, hgd_o, act_o, ig_o,
    wu, wu_sib, wd, wd_sib,
    xg, dyb, sa, ra, ah1, ahs, ar2, sb, rb, eg, actb, hgb, sg, gh1, ghs, gr2, igs,
    local_sem, ss, rs,
):
    r, c = lax.axis_index("row"), lax.axis_index("col")
    z, k = r // 2, r % 2
    other = 1 - k
    sign = 1 - 2 * k
    px, py = c // 4, c % 4

    def wrap(v):
        return lax.rem(v + NZ, NZ)

    def zdev(d):
        return {"row": wrap(z + d) * 2 + k, "col": c}

    def pcol(dx, dy):
        return lax.rem(px + dx, 4) * 4 + lax.rem(py + dy, 4)

    def pdev(dx, dy):
        return {"row": r, "col": pcol(dx, dy)}

    sib = {"row": z * 2 + other, "col": c}
    copies = []

    def send(src, dst, dev):
        n = len(copies)
        copy = pltpu.make_async_remote_copy(
            src_ref=src, dst_ref=dst, send_sem=ss.at[n], recv_sem=rs.at[n],
            device_id=dev, device_id_type=MESH,
        )
        copy.start()
        copies.append(copy)
        return copy

    def gather_start(buf):
        return {d: send(buf.at[z], buf.at[z], zdev(d)) for d in (6, -6, 3, -3, 1, -1)}

    def gather_relay(buf, first, d):
        first[d].wait_recv()
        block = wrap(z - d)
        return [send(buf.at[block], buf.at[block], zdev(e)) for e in (1, -1)]

    def gather_far(buf):
        block = wrap(z - 6 * sign)
        return [send(buf.at[block], buf.at[block], zdev(2 * sign))]

    def reduce_start(buf, h1):
        out = []
        for slot, d in enumerate((-2, -5, 4, 7, 1)):
            out.append(send(buf.at[wrap(z + d)], h1.at[slot], zdev(1)))
        for slot, d in enumerate((-4, -7, 2, 5, -1)):
            out.append(send(buf.at[wrap(z + d)], h1.at[5 + slot], zdev(-1)))
        out.append(send(buf.at[wrap(z + 8)], h1.at[10], zdev(-2 * sign)))
        return out

    def reduce_hub(buf, h1, hs, r2, first):
        for copy in first:
            copy.wait_recv()
        far = h1[10].astype(F32)
        second = []
        for slot, d in ((1, -6), (3, 6), (0, -3), (2, 3)):
            total = buf[wrap(z + d)].astype(F32) + h1[slot].astype(F32) + h1[5 + slot].astype(F32)
            if d == -6:
                total = total + jnp.where(k == 0, far, 0.0)
            if d == 6:
                total = total + jnp.where(k == 1, far, 0.0)
            hs[slot] = total.astype(BF16)
            second.append(send(hs.at[slot], r2.at[slot], zdev(d)))
        return second

    def reduce_end(buf, h1, r2, second):
        total = buf[z].astype(F32) + h1[4].astype(F32) + h1[9].astype(F32)
        for copy in second:
            copy.wait_recv()
        for slot in range(4):
            total = total + r2[slot].astype(F32)
        return total

    mine = pl.multiple_of(k * W, 16)
    theirs = pl.multiple_of(other * W, 16)
    load_wd = pltpu.make_async_copy(wd_hbm.at[pl.ds(mine, W)], wd, local_sem.at[0])
    load_wu = pltpu.make_async_copy(wu_hbm, wu, local_sem.at[1])
    load_wd.start()
    load_wu.start()

    dyb[k, c] = dy_ref[...]
    xg[k, z, 0:TD, :] = x_ref[...]
    xg[k, z, TD:16, :] = jnp.zeros((16 - TD, D2), BF16)

    barrier = pltpu.get_barrier_semaphore()
    partners = [pdev(*o) for o in PLANE] + [zdev(d) for d in (6, -6, 3, -3, 2, -2, 1, -1)] + [sib]
    for dev in partners:
        pl.semaphore_signal(barrier, inc=1, device_id=dev, device_id_type=MESH)
    pl.semaphore_wait(barrier, len(partners))

    dy_copies = {o: send(dyb.at[k, c], dyb.at[k, c], pdev(*o)) for o in PLANE}
    x_first = gather_start(xg.at[k])
    to_sib = [send(dyb.at[k, c], dyb.at[k, c], sib)]
    wd_copy = send(wd_hbm.at[pl.ds(theirs, W)], wd_sib, sib)
    wu_copy = send(wu_hbm.at[pl.ds(theirs, W)], wu_sib, sib)

    x_second = gather_relay(xg.at[k], x_first, 3) + gather_relay(xg.at[k], x_first, -3)
    for dx, dy in reversed(PLANE):
        dy_copies[dx, dy].wait_recv()
        block = pcol(4 - dx, 4 - dy)
        to_sib.append(send(dyb.at[k, block], dyb.at[k, block], sib))
    x_second += gather_relay(xg.at[k], x_first, 6) + gather_relay(xg.at[k], x_first, -6)
    x_second += gather_far(xg.at[k])

    load_wd.wait()
    wd_copy.wait_recv()
    for copy in to_sib:
        copy.wait_recv()
    a_copies = {}
    for dx in FAR_FIRST:
        g = lax.rem(px + dx, 4)
        own = dense(dyb[k, pl.ds(4 * g, 4)])
        dyd_o[pl.ds(pl.multiple_of(g * 96, 96), 96), :] = own
        part = dot_nt(own, wd[...]) + dot_nt(dense(dyb[other, pl.ds(4 * g, 4)]), wd_sib[...])
        for i in range(4):
            sa[4 * g + i] = part[TB * i : TB * (i + 1)].astype(BF16)
        for dy in FAR_FIRST:
            if (dx, dy) != (0, 0):
                a_copies[dx, dy] = send(sa.at[pcol(dx, dy)], ra.at[c], pdev(dx, dy))
    ra[c] = sa[c]

    load_wu.wait()
    x_first[1].wait_recv()
    x_first[-1].wait_recv()
    for copy in x_second:
        copy.wait_recv()
    x_sib = send(xg.at[k], xg.at[k], sib)
    x_sib.wait_recv()
    take0, take1 = unpad(0), unpad(1)
    b_copies = {}
    for dx in FAR_FIRST:
        g = lax.rem(px + dx, 4)
        part0 = xg[0, pl.ds(4 * g, 4)].reshape(64, D2)
        part1 = xg[1, pl.ds(4 * g, 4)].reshape(64, D2)
        own = (dot(take0, part0) + dot(take1, part1)).astype(BF16)
        xd_o[pl.ds(pl.multiple_of(g * 96, 96), 96), :] = own
        part = dot(own, wu[...])
        for i in range(4):
            sb[4 * g + i] = part[TB * i : TB * (i + 1)].astype(BF16)
        for dy in FAR_FIRST:
            if (dx, dy) != (0, 0):
                b_copies[dx, dy] = send(sb.at[pcol(dx, dy)], rb.at[c], pdev(dx, dy))
    rb[c] = sb[c]

    for copy in a_copies.values():
        copy.wait_recv()
    a_first = reduce_start(ra, ah1)

    for copy in b_copies.values():
        copy.wait_recv()
    hidden = jnp.zeros((TB, W), F32)
    for i in range(NP):
        hidden = hidden + rb[i].astype(F32)
    cdf, pdf = gelu_parts(hidden)
    eg[z] = (hidden * cdf).astype(BF16)
    slope = cdf + hidden * pdf
    e_first = gather_start(eg)

    a_second = reduce_hub(ra, ah1, ahs, ar2, a_first)
    e_second = []
    for d in (3, -3, 6, -6):
        e_second += gather_relay(eg, e_first, d)
    e_second += gather_far(eg)

    act_grad = reduce_end(ra, ah1, ar2, a_second)
    hgb[k, c] = (act_grad * slope).astype(BF16)
    f_copies = {o: send(hgb.at[k, c], hgb.at[k, c], pdev(*o)) for o in PLANE}
    to_sib = [send(hgb.at[k, c], hgb.at[k, c], sib)]

    e_first[1].wait_recv()
    e_first[-1].wait_recv()
    for copy in e_second:
        copy.wait_recv()
    e_copies = {o: send(eg.at[pcol(*o)], actb.at[k, c], pdev(*o)) for o in PLANE}
    actb[k, c] = eg[c]

    for dx, dy in reversed(PLANE):
        f_copies[dx, dy].wait_recv()
        block = pcol(4 - dx, 4 - dy)
        to_sib.append(send(hgb.at[k, block], hgb.at[k, block], sib))
    wu_copy.wait_recv()
    for copy in to_sib:
        copy.wait_recv()
    for g in range(4):
        own = dense(hgb[k, 4 * g : 4 * g + 4])
        hgd_o[96 * g : 96 * g + 96, :] = own
        part = dot_nt(own, wu[pl.ds(mine, W), :]) + dot_nt(
            dense(hgb[other, 4 * g : 4 * g + 4]), wu_sib[...]
        )
        for i in range(4):
            sg[4 * g + i] = part[TB * i : TB * (i + 1)].astype(BF16)
    g_first = reduce_start(sg, gh1)

    for copy in e_copies.values():
        copy.wait_recv()
    e_sib = send(actb.at[k], actb.at[k], sib)
    g_second = reduce_hub(sg, gh1, ghs, gr2, g_first)
    e_sib.wait_recv()
    for g in range(4):
        for h in range(2):
            act_o[h, 96 * g : 96 * g + 96, :] = dense(actb[h, 4 * g : 4 * g + 4])

    total = reduce_end(sg, gh1, gr2, g_second).astype(BF16)
    i = lax.broadcasted_iota(jnp.int32, (16, TB), 0)
    j = lax.broadcasted_iota(jnp.int32, (16, TB), 1)
    igs[k] = dot(jnp.where(j == i + TD * other, 1.0, 0.0).astype(BF16), total).astype(BF16)
    ig_sib = send(igs.at[k], igs.at[k], sib)
    ig_o[k] = dot(jnp.where(j == i + TD * k, 1.0, 0.0).astype(BF16), total).astype(BF16)
    ig_sib.wait_recv()
    ig_o[other] = igs[other]
    for copy in copies:
        copy.wait_send()


def shards(inputs, out_grad, w_up, w_down):
    vmem = pl.BlockSpec(memory_space=pltpu.VMEM)
    hbm = pl.BlockSpec(memory_space=pl.ANY)

    def blocks(*lead):
        return pltpu.VMEM((*lead, TB, W), BF16)

    xd, dyd, hgd, act, ig = pl.pallas_call(
        kernel,
        name="feed_forward_backward",
        out_shape=[
            jax.ShapeDtypeStruct((TOKENS, D2), BF16),
            jax.ShapeDtypeStruct((TOKENS, W), BF16),
            jax.ShapeDtypeStruct((TOKENS, W), BF16),
            jax.ShapeDtypeStruct((2, TOKENS, W), BF16),
            jax.ShapeDtypeStruct((2, 16, W), BF16),
        ],
        in_specs=[vmem, vmem, hbm, hbm],
        out_specs=[vmem] * 5,
        scratch_shapes=[
            pltpu.VMEM((D2, W), BF16), pltpu.VMEM((W, W), BF16), pltpu.VMEM((W, W), BF16), pltpu.VMEM((W, W), BF16),
            pltpu.VMEM((2, NZ, 16, D2), BF16), blocks(2, NP),
            blocks(NP), blocks(NP), blocks(11), blocks(4), blocks(4),
            blocks(NP), blocks(NP), blocks(NZ), blocks(2, NP), blocks(2, NP),
            blocks(NZ), blocks(11), blocks(4), blocks(4), pltpu.VMEM((2, 16, W), BF16),
            pltpu.SemaphoreType.DMA((2,)), pltpu.SemaphoreType.DMA((COPIES,)), pltpu.SemaphoreType.DMA((COPIES,)),
        ],
        compiler_params=pltpu.CompilerParams(
            collective_id=0, has_side_effects=True, vmem_limit_bytes=48 * 2**20
        ),
    )(inputs, out_grad, w_up, w_down)
    up_grad = dot_tn(xd, hgd)
    down_grad = jnp.concatenate([dot_tn(act[0], dyd), dot_tn(act[1], dyd)], axis=0)
    input_grad = jnp.concatenate([ig[0, :TD], ig[1, :TD]], axis=1)
    return (input_grad, up_grad, down_grad)


def solution(mesh):
    return jax.shard_map(
        shards,
        mesh=mesh,
        in_specs=(P("row", "col"), P("col", "row"), P("col", "row"), P("col", "row")),
        out_specs=(P("row", "col"), P("col", "row"), P("col", "row")),
        check_vma=False,
    )
```

```python
import math

import jax
import jax.numpy as jnp
from jax import lax
from jax.experimental import pallas as pl
from jax.experimental.pallas import tpu as pltpu
from jax.sharding import PartitionSpec as P

MESH = pl.DeviceIdType.MESH
BF16 = jnp.bfloat16
F32 = jnp.float32

NZ = 16
NP = 16
TB = 24
TD = 12
TOKENS = 384
W = 464
D2 = 928
COPIES = 240

PLANE = sorted(
    [(a, b) for a in range(4) for b in range(4) if (a, b) != (0, 0)],
    key=lambda o: -(min(o[0], 4 - o[0]) + min(o[1], 4 - o[1])),
)
FAR_FIRST = (2, 1, 3, 0)
NEAR_FIRST = (0, 1, 3, 2)
SLOTS = {
    -2: (0, 1), -5: (1, 1), 4: (2, 1), 7: (3, 1), 1: (4, 1),
    -4: (5, -1), -7: (6, -1), 2: (7, -1), 5: (8, -1), -1: (9, -1), 8: (10, 0),
}
ARRIVAL = ((0, 1, -1, 3), (-3, 2, -2, 4), (-4, 6, -6, 5), (-5, 7, -7, 8))


def dot(a, b):
    return jnp.dot(a, b, preferred_element_type=F32)


def dot_nt(a, b):
    return lax.dot_general(a, b, (((1,), (1,)), ((), ())), preferred_element_type=F32)


def dot_tn(a, b):
    return lax.dot_general(a, b, (((0,), (0,)), ((), ())), preferred_element_type=F32)


def dense(blocks):
    n, t, w = blocks.shape
    return blocks.astype(F32).reshape(n * t, w).astype(BF16)


def gelu_parts(hidden):
    cdf = 0.5 * (1.0 + lax.erf(hidden / math.sqrt(2.0)))
    pdf = jnp.exp(-0.5 * hidden * hidden) / math.sqrt(2.0 * math.pi)
    return (cdf, pdf)


def stack(blocks):
    return jnp.concatenate([block.astype(F32) for block in blocks], axis=0).astype(BF16)


def kernel(
    x_hbm, dy_hbm, wu_hbm, wd_hbm,
    xd_hbm, dyd_hbm, hgd_hbm, act_hbm, input_grad,
    act, wu, wu_sib, wd, wd_sib,
    xg, xd, dyd, hgd, dyb, sa, ra, ah1, ahs, ar2, sb, rb, eg, actb, hgb, sg, sgf, gh1, ghs, gr2, igs,
    local_sem, ss, rs, bss, brs,
):
    r, c = lax.axis_index("row"), lax.axis_index("col")
    z, k = r // 2, r % 2
    other = 1 - k
    sign = 1 - 2 * k
    px, py = c // 4, c % 4

    def wrap(v):
        return lax.rem(v + NZ, NZ)

    def zdev(d):
        return {"row": wrap(z + d) * 2 + k, "col": c}

    def pcol(dx, dy):
        return lax.rem(px + dx, 4) * 4 + lax.rem(py + dy, 4)

    def pdev(dx, dy):
        return {"row": r, "col": pcol(dx, dy)}

    sib = {"row": z * 2 + other, "col": c}
    copies = []

    def send(src, dst, dev):
        n = len(copies)
        copy = pltpu.make_async_remote_copy(
            src_ref=src, dst_ref=dst, send_sem=ss.at[n], recv_sem=rs.at[n],
            device_id=dev, device_id_type=MESH,
        )
        copy.start()
        copies.append(copy)
        return copy

    def gather_start(buf):
        return {-d: send(buf.at[z], buf.at[z], zdev(d)) for d in (6, -6, 3, -3, 1, -1)}

    def gather_relay(buf, got, d):
        got[d].wait_recv()
        block = wrap(z + d)
        for e in (1, -1):
            got[d - e] = send(buf.at[block], buf.at[block], zdev(e))

    def gather_far(buf, got):
        block = wrap(z - 6 * sign)
        got[8] = send(buf.at[block], buf.at[block], zdev(2 * sign))

    def reduce_start(buf, h1, ds=(8, -5, 7, -7, 5, -2, 4, -4, 2, 1, -1)):
        out = {}
        for d in ds:
            if d in SLOTS:
                slot, e = SLOTS[d]
                out[slot] = send(buf.at[wrap(z + d)], h1.at[slot], zdev(-2 * sign if d == 8 else e))
        return out

    def reduce_hub(buf, h1, hs, r2, first):
        first[10].wait_recv()
        far = h1[10].astype(F32)
        second = []
        for slot, d in ((1, -6), (3, 6), (0, -3), (2, 3)):
            first[slot].wait_recv()
            first[5 + slot].wait_recv()
            total = buf[wrap(z + d)].astype(F32) + h1[slot].astype(F32) + h1[5 + slot].astype(F32)
            if d == -6:
                total = total + jnp.where(k == 0, far, 0.0)
            if d == 6:
                total = total + jnp.where(k == 1, far, 0.0)
            hs[slot] = total.astype(BF16)
            second.append(send(hs.at[slot], r2.at[slot], zdev(d)))
        return second

    def reduce_end(buf, h1, r2, first, second):
        first[4].wait_recv()
        first[9].wait_recv()
        total = buf[z].astype(F32) + h1[4].astype(F32) + h1[9].astype(F32)
        for copy in second:
            copy.wait_recv()
        for slot in range(4):
            total = total + r2[slot].astype(F32)
        return total

    mine = pl.multiple_of(k * W, 16)
    theirs = pl.multiple_of(other * W, 16)
    load_x = pltpu.make_async_copy(x_hbm, xg.at[k, z], local_sem.at[0])
    load_dy = pltpu.make_async_copy(dy_hbm, dyb.at[k, c], local_sem.at[1])
    load_wd = pltpu.make_async_copy(wd_hbm.at[pl.ds(mine, W)], wd, local_sem.at[2])
    load_wu = pltpu.make_async_copy(wu_hbm, wu, local_sem.at[3])
    load_x.start()
    load_dy.start()
    load_wd.start()
    load_wu.start()

    barrier = pltpu.get_barrier_semaphore()
    partners = [pdev(*o) for o in PLANE] + [zdev(d) for d in (6, -6, 3, -3, 2, -2, 1, -1)] + [sib]
    for dev in partners:
        pl.semaphore_signal(barrier, inc=1, device_id=dev, device_id_type=MESH)
    load_x.wait()
    load_dy.wait()
    pl.semaphore_wait(barrier, len(partners))

    dy_copies = {o: send(dyb.at[k, c], dyb.at[k, c], pdev(*o)) for o in PLANE}
    x_got = gather_start(xg.at[k])
    to_sib = {0: [send(dyb.at[k, c], dyb.at[k, c], sib)], 1: [], 2: [], 3: []}
    x_sib = {0: send(xg.at[k, z], xg.at[k, z], sib)}
    wd_copy = send(wd_hbm.at[pl.ds(theirs, W)], wd_sib, sib)
    wu_copy = send(wu_hbm.at[pl.ds(theirs, W)], wu_sib, sib)

    a_copies = {}

    def forward(dx):
        for dy in NEAR_FIRST:
            if (dx, dy) != (0, 0):
                dy_copies[dx, dy].wait_recv()
                block = pcol(4 - dx, 4 - dy)
                to_sib[dx].append(send(dyb.at[k, block], dyb.at[k, block], sib))

    def act_part(dx):
        for copy in to_sib[dx]:
            copy.wait_recv()
        g = lax.rem(px + 4 - dx, 4)
        own = dense(dyb[k, pl.ds(4 * g, 4)])
        dyd[pl.ds(pl.multiple_of(g * 96, 96), 96), :] = own
        part = dot_nt(own, wd[...]) + dot_nt(dense(dyb[other, pl.ds(4 * g, 4)]), wd_sib[...])
        for i in range(4):
            sa[4 * g + i] = part[TB * i : TB * (i + 1)].astype(BF16)
        for dy in FAR_FIRST:
            if (dx, dy) != (0, 0):
                to = (4 - dx) % 4, dy
                a_copies[to] = send(sa.at[pcol(*to)], ra.at[c], pdev(*to))

    b_copies = []

    def x_forward(*ds):
        for d in ds:
            if d not in (3, -3, 6, -6):
                x_got[d].wait_recv()
            block = wrap(z + d)
            x_sib[d] = send(xg.at[k, block], xg.at[k, block], sib)

    def hidden_part(n):
        for d in ARRIVAL[n]:
            x_sib[d].wait_recv()
        blocks = [wrap(z + d) for d in ARRIVAL[n]]
        own = stack([xg[core, block] for block in blocks for core in range(2)])
        xd[96 * n : 96 * n + 96, :] = own
        part = dot(own, wu[...])
        for i, block in enumerate(blocks):
            sb[block] = part[TB * i : TB * (i + 1)].astype(BF16)
        for i, block in enumerate(blocks):
            there = pltpu.make_async_remote_copy(
                src_ref=sb.at[block], dst_ref=rb.at[c], send_sem=bss.at[4 * n + i], recv_sem=brs.at[c],
                device_id={"row": r, "col": block}, device_id_type=MESH,
            )
            here = pltpu.make_async_copy(sb.at[block], rb.at[c], brs.at[c])
            pl.when(block != c)(there.start)
            pl.when(block == c)(here.start)
            b_copies.append((block, there))

    forward(0)
    x_forward(1, -1)
    gather_relay(xg.at[k], x_got, 3)
    gather_relay(xg.at[k], x_got, -3)
    forward(1)
    load_wd.wait()
    wd_copy.wait_recv()
    act_part(0)
    forward(3)
    act_part(1)
    x_forward(3, -3)
    forward(2)
    act_part(3)
    gather_relay(xg.at[k], x_got, 6)
    gather_relay(xg.at[k], x_got, -6)
    gather_far(xg.at[k], x_got)
    act_part(2)
    ra[c] = sa[c]
    x_forward(2, -2, 4, -4, 6, -6)
    load_wu.wait()
    hidden_part(0)
    hidden_part(1)
    x_forward(5, -5, 7, -7, 8)
    hidden_part(2)
    hidden_part(3)

    for copy in a_copies.values():
        copy.wait_recv()
    a_first = reduce_start(ra, ah1)
    a_second = reduce_hub(ra, ah1, ahs, ar2, a_first)

    for j in range(NP):
        pltpu.make_async_remote_copy(
            src_ref=sb.at[j], dst_ref=rb.at[j], send_sem=bss.at[j], recv_sem=brs.at[j],
            device_id=sib, device_id_type=MESH,
        ).wait_recv()
    hidden = jnp.zeros((TB, W), F32)
    for i in range(NP):
        hidden = hidden + rb[i].astype(F32)
    cdf, pdf = gelu_parts(hidden)
    eg[z] = (hidden * cdf).astype(BF16)
    slope = cdf + hidden * pdf

    act_grad = reduce_end(ra, ah1, ar2, a_first, a_second)
    hgb[k, c] = (act_grad * slope).astype(BF16)
    f_copies = {o: send(hgb.at[k, c], hgb.at[k, c], pdev(*o)) for o in PLANE}
    f_sib = [send(hgb.at[k, c], hgb.at[k, c], sib)]
    e_got = gather_start(eg)

    def f_forward(offsets):
        for dx, dy in offsets:
            f_copies[dx, dy].wait_recv()
            block = pcol(4 - dx, 4 - dy)
            f_sib.append(send(hgb.at[k, block], hgb.at[k, block], sib))

    f_forward(PLANE[:4:-1])
    gather_relay(eg, e_got, 3)
    gather_relay(eg, e_got, -3)
    f_forward(PLANE[4::-1])
    wu_copy.wait_recv()
    for copy in f_sib:
        copy.wait_recv()
    g_first = {}
    for n in (3, 2, 1, 0):
        blocks = [wrap(z + d) for d in ARRIVAL[n]]
        own = stack([hgb[k, block] for block in blocks])
        hgd[96 * n : 96 * n + 96, :] = own
        part = dot_nt(own, wu[pl.ds(mine, W), :]) + dot_nt(
            stack([hgb[other, block] for block in blocks]), wu_sib[...]
        )
        for i, block in enumerate(blocks):
            sgf[block] = part[TB * i : TB * (i + 1)]
            sg[block] = part[TB * i : TB * (i + 1)].astype(BF16)
        g_first |= reduce_start(sg, gh1, ARRIVAL[n])
        if n == 3:
            gather_relay(eg, e_got, 6)
            gather_relay(eg, e_got, -6)
            gather_far(eg, e_got)

    g_second = reduce_hub(sgf, gh1, ghs, gr2, g_first)
    for d in (1, -1, 2, -2, 4, -4, 5, -5, 7, -7, 8):
        e_got[d].wait_recv()
    e_copies = [send(eg.at[pcol(*o)], actb.at[k, c], pdev(*o)) for o in PLANE]
    actb[k, c] = eg[c]

    flush = [pltpu.make_async_copy(xd, xd_hbm, local_sem.at[4])]
    flush.append(pltpu.make_async_copy(hgd, hgd_hbm, local_sem.at[5]))
    flush.append(pltpu.make_async_copy(dyd, dyd_hbm, local_sem.at[6]))
    for copy in flush:
        copy.start()
    for copy in e_copies:
        copy.wait_recv()
    e_sib = send(actb.at[k], actb.at[k], sib)
    act[k] = dense(actb[k])
    e_sib.wait_recv()
    act[other] = dense(actb[other])
    flush.append(pltpu.make_async_copy(act, act_hbm, local_sem.at[7]))
    flush[3].start()

    total = reduce_end(sgf, gh1, gr2, g_first, g_second).astype(BF16)
    i = lax.broadcasted_iota(jnp.int32, (16, TB), 0)
    j = lax.broadcasted_iota(jnp.int32, (16, TB), 1)
    igs[k] = dot(jnp.where(j == i + TD * other, 1.0, 0.0).astype(BF16), total).astype(BF16)
    ig_sib = send(igs.at[k], igs.at[k], sib)
    kept = dot(jnp.where(j == i + TD * k, 1.0, 0.0).astype(BF16), total)
    ig_sib.wait_recv()
    came = igs[other].astype(F32)
    halves = [jnp.where(k == 0, kept, came), jnp.where(k == 0, came, kept)]
    input_grad[...] = jnp.concatenate(halves, axis=1)[:TD].astype(BF16)
    for copy in flush:
        copy.wait()
    for copy in copies:
        copy.wait_send()
    for block, there in b_copies:
        pl.when(block != c)(there.wait_send)


def products(
    xd_hbm, dyd_hbm, hgd_hbm, act_hbm, ig_hbm, ig_out, up_hbm, down_hbm,
    xd, dyd, hgd, act, ig, up, down, load_sems, sems,
):
    pairs = ((ig_hbm, ig), (xd_hbm, xd), (hgd_hbm, hgd), (act_hbm, act), (dyd_hbm, dyd))
    loads = [pltpu.make_async_copy(a, b, load_sems.at[n]) for n, (a, b) in enumerate(pairs)]
    for load in loads:
        load.start()
    copies = []

    def write(src, dst):
        copies.append(pltpu.make_async_copy(src, dst, sems.at[len(copies)]))
        copies[-1].start()

    loads[0].wait()
    write(ig, ig_out)
    loads[1].wait()
    loads[2].wait()
    for low, high in ((0, 512), (512, D2)):
        up[low:high, :] = dot_tn(xd[:, low:high], hgd[...])
        write(up.at[low:high], up_hbm.at[low:high])
    loads[3].wait()
    loads[4].wait()
    for n in range(2):
        down[n * W : n * W + W, :] = dot_tn(act[n], dyd[...])
        write(down.at[n * W : n * W + W], down_hbm.at[n * W : n * W + W])
    for copy in copies:
        copy.wait()


def shards(inputs, out_grad, w_up, w_down):
    vmem = pl.BlockSpec(memory_space=pltpu.VMEM)
    hbm = pl.BlockSpec(memory_space=pltpu.HBM)

    def blocks(*lead):
        return pltpu.VMEM((*lead, TB, W), BF16)

    gathered = pl.pallas_call(
        kernel,
        name="feed_forward_backward",
        out_shape=[
            jax.ShapeDtypeStruct((TOKENS, D2), BF16),
            jax.ShapeDtypeStruct((TOKENS, W), BF16),
            jax.ShapeDtypeStruct((TOKENS, W), BF16),
            jax.ShapeDtypeStruct((2, TOKENS, W), BF16),
            jax.ShapeDtypeStruct((TD, D2), BF16),
        ],
        in_specs=[hbm] * 4,
        out_specs=[hbm] * 4 + [vmem],
        scratch_shapes=[
            pltpu.VMEM((2, TOKENS, W), BF16), pltpu.VMEM((D2, W), BF16), pltpu.VMEM((W, W), BF16), pltpu.VMEM((W, W), BF16), pltpu.VMEM((W, W), BF16),
            pltpu.VMEM((2, NZ, TD, D2), BF16), pltpu.VMEM((TOKENS, D2), BF16),
            pltpu.VMEM((TOKENS, W), BF16), pltpu.VMEM((TOKENS, W), BF16), blocks(2, NP),
            blocks(NP), blocks(NP), blocks(11), blocks(4), blocks(4),
            blocks(NP), blocks(NP), blocks(NZ), blocks(2, NP), blocks(2, NP),
            blocks(NZ), pltpu.VMEM((NZ, TB, W), F32), blocks(11), blocks(4), blocks(4),
            pltpu.VMEM((2, 16, W), BF16),
            pltpu.SemaphoreType.DMA((8,)), pltpu.SemaphoreType.DMA((COPIES,)), pltpu.SemaphoreType.DMA((COPIES,)),
            pltpu.SemaphoreType.DMA((NP,)), pltpu.SemaphoreType.DMA((NP,)),
        ],
        compiler_params=pltpu.CompilerParams(
            collective_id=0, has_side_effects=True, vmem_limit_bytes=60 * 2**20
        ),
    )(inputs, out_grad, w_up, w_down)
    return pl.pallas_call(
        products,
        name="weight_gradients",
        out_shape=[
            jax.ShapeDtypeStruct((TD, D2), BF16),
            jax.ShapeDtypeStruct((D2, W), F32),
            jax.ShapeDtypeStruct((D2, W), F32),
        ],
        in_specs=[hbm] * 5,
        out_specs=[hbm] * 3,
        scratch_shapes=[
            pltpu.VMEM((TOKENS, D2), BF16), pltpu.VMEM((TOKENS, W), BF16), pltpu.VMEM((TOKENS, W), BF16),
            pltpu.VMEM((2, TOKENS, W), BF16), pltpu.VMEM((TD, D2), BF16),
            pltpu.VMEM((D2, W), F32), pltpu.VMEM((D2, W), F32),
            pltpu.SemaphoreType.DMA((5,)), pltpu.SemaphoreType.DMA((5,)),
        ],
        compiler_params=pltpu.CompilerParams(vmem_limit_bytes=60 * 2**20),
    )(*gathered)


def solution(mesh):
    return jax.shard_map(
        shards,
        mesh=mesh,
        in_specs=(P("row", "col"), P("col", "row"), P("col", "row"), P("col", "row")),
        out_specs=(P("row", "col"), P("col", "row"), P("col", "row")),
        check_vma=False,
    )
```

```python
import math

import jax
import jax.numpy as jnp
from jax import lax
from jax.experimental import pallas as pl
from jax.experimental.pallas import tpu as pltpu
from jax.sharding import PartitionSpec as P

MESH = pl.DeviceIdType.MESH
BF16 = jnp.bfloat16
F32 = jnp.float32

NZ = 16
NP = 16
TB = 24
TD = 12
TOKENS = 384
W = 464
D2 = 928
COPIES = 240

PLANE = sorted(
    [(a, b) for a in range(4) for b in range(4) if (a, b) != (0, 0)],
    key=lambda o: -(min(o[0], 4 - o[0]) + min(o[1], 4 - o[1])),
)
FAR_FIRST = (2, 1, 3, 0)
NEAR_FIRST = (0, 1, 3, 2)
SLOTS = {
    -2: (0, 1), -5: (1, 1), 4: (2, 1), 7: (3, 1), 1: (4, 1),
    -4: (5, -1), -7: (6, -1), 2: (7, -1), 5: (8, -1), -1: (9, -1), 8: (10, 0),
}
ARRIVAL = ((0, 1, -1, 3), (-3, 2, -2, 4), (-4, 6, -6, 5), (-5, 7, -7, 8))


def dot(a, b):
    return jnp.dot(a, b, preferred_element_type=F32)


def dot_nt(a, b):
    return lax.dot_general(a, b, (((1,), (1,)), ((), ())), preferred_element_type=F32)


def dense(blocks):
    n, t, w = blocks.shape
    return blocks.astype(F32).reshape(n * t, w).astype(BF16)


def gelu_parts(hidden):
    cdf = 0.5 * (1.0 + lax.erf(hidden / math.sqrt(2.0)))
    pdf = jnp.exp(-0.5 * hidden * hidden) / math.sqrt(2.0 * math.pi)
    return (cdf, pdf)


def stack(blocks):
    return jnp.concatenate([block.astype(F32) for block in blocks], axis=0).astype(BF16)


def kernel(
    x_hbm, dy_hbm, wu_hbm, wd_hbm,
    xd_hbm, dyd_hbm, hgd_hbm, act_hbm, input_grad,
    act, xdt, wu, wu_sib, wd, wd_sib,
    xg, xd, dyd, hgd, dyb, sa, ra, ah1, ahs, ar2, sb, rb, eg, actb, hgb, sg, sgf, gh1, ghs, gr2, igs,
    local_sem, ss, rs, bss, brs, ess, ers, ass, ars,
):
    r, c = lax.axis_index("row"), lax.axis_index("col")
    z, k = r // 2, r % 2
    other = 1 - k
    sign = 1 - 2 * k
    px, py = c // 4, c % 4

    def wrap(v):
        return lax.rem(v + NZ, NZ)

    def zdev(d):
        return {"row": wrap(z + d) * 2 + k, "col": c}

    def pcol(dx, dy):
        return lax.rem(px + dx, 4) * 4 + lax.rem(py + dy, 4)

    def pdev(dx, dy):
        return {"row": r, "col": pcol(dx, dy)}

    sib = {"row": z * 2 + other, "col": c}
    copies = []

    def send(src, dst, dev):
        n = len(copies)
        copy = pltpu.make_async_remote_copy(
            src_ref=src, dst_ref=dst, send_sem=ss.at[n], recv_sem=rs.at[n],
            device_id=dev, device_id_type=MESH,
        )
        copy.start()
        copies.append(copy)
        return copy

    maybe = []

    def send_column(src, dst, col, sends, n, recvs):
        there = pltpu.make_async_remote_copy(
            src_ref=src, dst_ref=dst.at[c], send_sem=sends.at[n], recv_sem=recvs.at[c],
            device_id={"row": r, "col": col}, device_id_type=MESH,
        )
        here = pltpu.make_async_copy(src, dst.at[c], recvs.at[c])
        pl.when(col != c)(there.start)
        pl.when(col == c)(here.start)
        maybe.append((col != c, there))

    def wait_columns(dst, sends, recvs):
        for j in range(NP):
            pltpu.make_async_remote_copy(
                src_ref=dst.at[j], dst_ref=dst.at[j], send_sem=sends.at[j], recv_sem=recvs.at[j],
                device_id=sib, device_id_type=MESH,
            ).wait_recv()

    def gather_start(buf):
        return {-d: send(buf.at[z], buf.at[z], zdev(d)) for d in (6, -6, 3, -3, 1, -1)}

    def gather_relay(buf, got, d):
        got[d].wait_recv()
        block = wrap(z + d)
        for e in (1, -1):
            got[d - e] = send(buf.at[block], buf.at[block], zdev(e))

    def gather_far(buf, got):
        block = wrap(z - 6 * sign)
        got[8] = send(buf.at[block], buf.at[block], zdev(2 * sign))

    def reduce_start(buf, h1, ds=(8, -5, 7, -7, 5, -2, 4, -4, 2, 1, -1)):
        out = {}
        for d in ds:
            if d in SLOTS:
                slot, e = SLOTS[d]
                out[slot] = send(buf.at[wrap(z + d)], h1.at[slot], zdev(-2 * sign if d == 8 else e))
        return out

    def reduce_hub(buf, h1, hs, r2, first):
        first[10].wait_recv()
        far = h1[10].astype(F32)
        second = []
        for slot, d in ((1, -6), (3, 6), (0, -3), (2, 3)):
            first[slot].wait_recv()
            first[5 + slot].wait_recv()
            total = buf[wrap(z + d)].astype(F32) + h1[slot].astype(F32) + h1[5 + slot].astype(F32)
            if d == -6:
                total = total + jnp.where(k == 0, far, 0.0)
            if d == 6:
                total = total + jnp.where(k == 1, far, 0.0)
            hs[slot] = total.astype(BF16)
            second.append(send(hs.at[slot], r2.at[slot], zdev(d)))
        return second

    def reduce_end(buf, h1, r2, first, second):
        first[4].wait_recv()
        first[9].wait_recv()
        total = buf[z].astype(F32) + h1[4].astype(F32) + h1[9].astype(F32)
        for copy in second:
            copy.wait_recv()
        for slot in range(4):
            total = total + r2[slot].astype(F32)
        return total

    mine = pl.multiple_of(k * W, 16)
    theirs = pl.multiple_of(other * W, 16)
    load_x = pltpu.make_async_copy(x_hbm, xg.at[k, z], local_sem.at[0])
    load_dy = pltpu.make_async_copy(dy_hbm, dyb.at[k, c], local_sem.at[1])
    load_wd = pltpu.make_async_copy(wd_hbm.at[pl.ds(mine, W)], wd, local_sem.at[2])
    load_wu = pltpu.make_async_copy(wu_hbm, wu, local_sem.at[3])
    load_x.start()
    load_dy.start()
    load_wd.start()
    load_wu.start()

    barrier = pltpu.get_barrier_semaphore()
    partners = [zdev(d) for d in (6, -6)] + [pdev(*o) for o in PLANE] + [zdev(d) for d in (3, -3, 2, -2, 1, -1)] + [sib]
    for dev in partners:
        pl.semaphore_signal(barrier, inc=1, device_id=dev, device_id_type=MESH)
    load_x.wait()
    load_dy.wait()
    pl.semaphore_wait(barrier, len(partners))

    x_got = gather_start(xg.at[k])
    dy_copies = {o: send(dyb.at[k, c], dyb.at[k, c], pdev(*o)) for o in PLANE}
    to_sib = {0: [send(dyb.at[k, c], dyb.at[k, c], sib)], 1: [], 2: [], 3: []}
    x_sib = {0: send(xg.at[k, z], xg.at[k, z], sib)}
    wd_copy = send(wd_hbm.at[pl.ds(theirs, W)], wd_sib, sib)
    wu_copy = send(wu_hbm.at[pl.ds(theirs, W)], wu_sib, sib)

    a_copies = {}

    def forward(dx):
        for dy in NEAR_FIRST:
            if (dx, dy) != (0, 0):
                dy_copies[dx, dy].wait_recv()
                block = pcol(4 - dx, 4 - dy)
                to_sib[dx].append(send(dyb.at[k, block], dyb.at[k, block], sib))

    def act_part(dx):
        for copy in to_sib[dx]:
            copy.wait_recv()
        g = lax.rem(px + 4 - dx, 4)
        own = dense(dyb[k, pl.ds(4 * g, 4)])
        dyd[pl.ds(pl.multiple_of(g * 96, 96), 96), :] = own
        part = dot_nt(own, wd[...]) + dot_nt(dense(dyb[other, pl.ds(4 * g, 4)]), wd_sib[...])
        for i in range(4):
            sa[4 * g + i] = part[TB * i : TB * (i + 1)].astype(BF16)
        for dy in FAR_FIRST:
            if (dx, dy) != (0, 0):
                to = (4 - dx) % 4, dy
                a_copies[to] = send(sa.at[pcol(*to)], ra.at[c], pdev(*to))


    def x_forward(*ds):
        for d in ds:
            if d not in (3, -3, 6, -6):
                x_got[d].wait_recv()
            block = wrap(z + d)
            x_sib[d] = send(xg.at[k, block], xg.at[k, block], sib)

    def hidden_part(n):
        for d in ARRIVAL[n]:
            x_sib[d].wait_recv()
        blocks = [wrap(z + d) for d in ARRIVAL[n]]
        own = stack([xg[core, block] for block in blocks for core in range(2)])
        xd[96 * n : 96 * n + 96, :] = own
        part = dot(own, wu[...])
        for i, block in enumerate(blocks):
            sb[block] = part[TB * i : TB * (i + 1)].astype(BF16)
        for i, block in enumerate(blocks):
            send_column(sb.at[block], rb, block, bss, 4 * n + i, brs)

    forward(0)
    x_forward(1, -1)
    gather_relay(xg.at[k], x_got, 3)
    gather_relay(xg.at[k], x_got, -3)
    forward(1)
    load_wd.wait()
    wd_copy.wait_recv()
    act_part(0)
    forward(3)
    act_part(1)
    x_forward(3, -3)
    forward(2)
    gather_relay(xg.at[k], x_got, 6)
    gather_relay(xg.at[k], x_got, -6)
    gather_far(xg.at[k], x_got)
    act_part(3)
    act_part(2)
    ra[c] = sa[c]
    x_forward(2, -2, 4, -4, 6, -6)
    load_wu.wait()
    hidden_part(0)
    hidden_part(1)
    x_forward(5, -5, 7, -7, 8)
    hidden_part(2)
    hidden_part(3)

    a_first = {}
    for d, (slot, e) in SLOTS.items():
        a_first[slot] = pltpu.make_async_remote_copy(
            src_ref=ra.at[wrap(z + d)], dst_ref=ah1.at[slot], send_sem=ass.at[slot], recv_sem=ars.at[slot],
            device_id=zdev(-2 * sign if d == 8 else e), device_id_type=MESH,
        )

    def pass_on(block):
        for d, (slot, _) in SLOTS.items():
            pl.when(block == wrap(z + d))(a_first[slot].start)

    pass_on(c)
    for dx, dy in reversed(PLANE):
        a_copies[dx, dy].wait_recv()
        pass_on(pcol(4 - dx, 4 - dy))
    a_second = reduce_hub(ra, ah1, ahs, ar2, a_first)

    wait_columns(rb, bss, brs)
    hidden = jnp.zeros((TB, W), F32)
    for i in range(NP):
        hidden = hidden + rb[i].astype(F32)
    cdf, pdf = gelu_parts(hidden)
    eg[z] = (hidden * cdf).astype(BF16)
    slope = cdf + hidden * pdf

    act_grad = reduce_end(ra, ah1, ar2, a_first, a_second)
    hgb[k, c] = (act_grad * slope).astype(BF16)
    f_copies = {o: send(hgb.at[k, c], hgb.at[k, c], pdev(*o)) for o in PLANE}
    f_sib = [send(hgb.at[k, c], hgb.at[k, c], sib)]
    e_got = gather_start(eg)

    def e_send(*ds):
        for d in ds:
            if d not in (0, 3, -3, 6, -6):
                e_got[d].wait_recv()
            block = wrap(z + d)
            send_column(eg.at[block], actb.at[k], block, ess, d + 7, ers)

    def f_forward(offsets):
        for dx, dy in offsets:
            f_copies[dx, dy].wait_recv()
            block = pcol(4 - dx, 4 - dy)
            f_sib.append(send(hgb.at[k, block], hgb.at[k, block], sib))

    f_forward(reversed(PLANE))
    gather_relay(eg, e_got, 3)
    gather_relay(eg, e_got, -3)
    wu_copy.wait_recv()
    for copy in f_sib:
        copy.wait_recv()
    g_first = {}
    for n in (3, 2, 1, 0):
        blocks = [wrap(z + d) for d in ARRIVAL[n]]
        own = stack([hgb[k, block] for block in blocks])
        hgd[96 * n : 96 * n + 96, :] = own
        part = dot_nt(own, wu[pl.ds(mine, W), :]) + dot_nt(
            stack([hgb[other, block] for block in blocks]), wu_sib[...]
        )
        for i, block in enumerate(blocks):
            sgf[block] = part[TB * i : TB * (i + 1)]
            sg[block] = part[TB * i : TB * (i + 1)].astype(BF16)
        g_first |= reduce_start(sg, gh1, ARRIVAL[n])
        if n == 3:
            gather_relay(eg, e_got, 6)
            gather_relay(eg, e_got, -6)
            gather_far(eg, e_got)
        if n == 2:
            e_send(0, 3, -3, 6, -6, 1, -1)
    e_send(2, -2, 4, -4)

    g_second = reduce_hub(sgf, gh1, ghs, gr2, g_first)
    e_send(5, -5, 7, -7, 8)
    xdt[...] = xd[...].T
    flush = [pltpu.make_async_copy(xdt, xd_hbm, local_sem.at[4])]
    flush.append(pltpu.make_async_copy(hgd, hgd_hbm, local_sem.at[5]))
    flush.append(pltpu.make_async_copy(dyd, dyd_hbm, local_sem.at[6]))
    for copy in flush:
        copy.start()
    wait_columns(actb.at[k], ess, ers)
    e_sib = send(actb.at[k], actb.at[k], sib)
    act[pl.ds(mine, W), :] = dense(actb[k]).T
    e_sib.wait_recv()
    act[pl.ds(theirs, W), :] = dense(actb[other]).T
    flush.append(pltpu.make_async_copy(act, act_hbm, local_sem.at[7]))
    flush[3].start()

    total = reduce_end(sgf, gh1, gr2, g_first, g_second).astype(BF16)
    i = lax.broadcasted_iota(jnp.int32, (16, TB), 0)
    j = lax.broadcasted_iota(jnp.int32, (16, TB), 1)
    igs[k] = dot(jnp.where(j == i + TD * other, 1.0, 0.0).astype(BF16), total).astype(BF16)
    ig_sib = send(igs.at[k], igs.at[k], sib)
    kept = dot(jnp.where(j == i + TD * k, 1.0, 0.0).astype(BF16), total)
    ig_sib.wait_recv()
    came = igs[other].astype(F32)
    halves = [jnp.where(k == 0, kept, came), jnp.where(k == 0, came, kept)]
    input_grad[...] = jnp.concatenate(halves, axis=1)[:TD].astype(BF16)
    for copy in flush:
        copy.wait()
    for copy in [*copies, *a_first.values()]:
        copy.wait_send()
    for sent, there in maybe:
        pl.when(sent)(there.wait_send)


def products(
    xd_hbm, dyd_hbm, hgd_hbm, act_hbm, ig_hbm, ig_out, up_hbm, down_hbm,
    xd, dyd, hgd, act, ig, up, down, load_sems, sems,
):
    pairs = ((ig_hbm, ig), (xd_hbm, xd), (hgd_hbm, hgd), (act_hbm, act), (dyd_hbm, dyd))
    loads = [pltpu.make_async_copy(a, b, load_sems.at[n]) for n, (a, b) in enumerate(pairs)]
    for load in loads:
        load.start()
    copies = []

    def write(src, dst):
        copies.append(pltpu.make_async_copy(src, dst, sems.at[len(copies)]))
        copies[-1].start()

    loads[0].wait()
    write(ig, ig_out)
    loads[1].wait()
    loads[2].wait()
    for low, high in ((0, 512), (512, D2)):
        up[low:high, :] = dot(xd[low:high, :], hgd[...])
        write(up.at[low:high], up_hbm.at[low:high])
    loads[3].wait()
    loads[4].wait()
    for n in range(2):
        down[n * W : n * W + W, :] = dot(act[n * W : n * W + W, :], dyd[...])
        write(down.at[n * W : n * W + W], down_hbm.at[n * W : n * W + W])
    for copy in copies:
        copy.wait()


def shards(inputs, out_grad, w_up, w_down):
    vmem = pl.BlockSpec(memory_space=pltpu.VMEM)
    hbm = pl.BlockSpec(memory_space=pltpu.HBM)

    def blocks(*lead):
        return pltpu.VMEM((*lead, TB, W), BF16)

    gathered = pl.pallas_call(
        kernel,
        name="feed_forward_backward",
        out_shape=[
            jax.ShapeDtypeStruct((D2, TOKENS), BF16),
            jax.ShapeDtypeStruct((TOKENS, W), BF16),
            jax.ShapeDtypeStruct((TOKENS, W), BF16),
            jax.ShapeDtypeStruct((D2, TOKENS), BF16),
            jax.ShapeDtypeStruct((TD, D2), BF16),
        ],
        in_specs=[hbm] * 4,
        out_specs=[hbm] * 4 + [vmem],
        scratch_shapes=[
            pltpu.VMEM((D2, TOKENS), BF16), pltpu.VMEM((D2, TOKENS), BF16), pltpu.VMEM((D2, W), BF16), pltpu.VMEM((W, W), BF16), pltpu.VMEM((W, W), BF16), pltpu.VMEM((W, W), BF16),
            pltpu.VMEM((2, NZ, TD, D2), BF16), pltpu.VMEM((TOKENS, D2), BF16),
            pltpu.VMEM((TOKENS, W), BF16), pltpu.VMEM((TOKENS, W), BF16), blocks(2, NP),
            blocks(NP), blocks(NP), blocks(11), blocks(4), blocks(4),
            blocks(NP), blocks(NP), blocks(NZ), blocks(2, NP), blocks(2, NP),
            blocks(NZ), pltpu.VMEM((NZ, TB, W), F32), blocks(11), blocks(4), blocks(4),
            pltpu.VMEM((2, 16, W), BF16),
            pltpu.SemaphoreType.DMA((8,)), pltpu.SemaphoreType.DMA((COPIES,)), pltpu.SemaphoreType.DMA((COPIES,)),
            pltpu.SemaphoreType.DMA((NP,)), pltpu.SemaphoreType.DMA((NP,)),
            pltpu.SemaphoreType.DMA((NP,)), pltpu.SemaphoreType.DMA((NP,)),
            pltpu.SemaphoreType.DMA((11,)), pltpu.SemaphoreType.DMA((11,)),
        ],
        compiler_params=pltpu.CompilerParams(
            collective_id=0, has_side_effects=True, vmem_limit_bytes=60 * 2**20
        ),
    )(inputs, out_grad, w_up, w_down)
    return pl.pallas_call(
        products,
        name="weight_gradients",
        out_shape=[
            jax.ShapeDtypeStruct((TD, D2), BF16),
            jax.ShapeDtypeStruct((D2, W), F32),
            jax.ShapeDtypeStruct((D2, W), F32),
        ],
        in_specs=[hbm] * 5,
        out_specs=[hbm] * 3,
        scratch_shapes=[
            pltpu.VMEM((D2, TOKENS), BF16), pltpu.VMEM((TOKENS, W), BF16), pltpu.VMEM((TOKENS, W), BF16),
            pltpu.VMEM((D2, TOKENS), BF16), pltpu.VMEM((TD, D2), BF16),
            pltpu.VMEM((D2, W), F32), pltpu.VMEM((D2, W), F32),
            pltpu.SemaphoreType.DMA((5,)), pltpu.SemaphoreType.DMA((5,)),
        ],
        compiler_params=pltpu.CompilerParams(vmem_limit_bytes=60 * 2**20),
    )(*gathered)


def solution(mesh):
    return jax.shard_map(
        shards,
        mesh=mesh,
        in_specs=(P("row", "col"), P("col", "row"), P("col", "row"), P("col", "row")),
        out_specs=(P("row", "col"), P("col", "row"), P("col", "row")),
        check_vma=False,
    )
```

```python
import math

import jax
import jax.numpy as jnp
from jax import lax
from jax.experimental import pallas as pl
from jax.experimental.pallas import tpu as pltpu
from jax.sharding import PartitionSpec as P

MESH = pl.DeviceIdType.MESH
BF16 = jnp.bfloat16
F32 = jnp.float32

NZ = 16
NP = 16
TB = 24
TD = 12
TOKENS = 384
W = 464
D2 = 928
COPIES = 240

PLANE = sorted(
    [(a, b) for a in range(4) for b in range(4) if (a, b) != (0, 0)],
    key=lambda o: -(min(o[0], 4 - o[0]) + min(o[1], 4 - o[1])),
)
FAR_FIRST = (2, 1, 3, 0)
NEAR_FIRST = (0, 1, 3, 2)
SLOTS = {
    -2: (0, 1), -5: (1, 1), 4: (2, 1), 7: (3, 1), 1: (4, 1),
    -4: (5, -1), -7: (6, -1), 2: (7, -1), 5: (8, -1), -1: (9, -1), 8: (10, 0),
}
ARRIVAL = ((0, 1, -1, 3), (-3, 2, -2, 4), (-4, 6, -6, 5), (-5, 7, -7, 8))


def dot(a, b):
    return jnp.dot(a, b, preferred_element_type=F32)


def dot_nt(a, b):
    return lax.dot_general(a, b, (((1,), (1,)), ((), ())), preferred_element_type=F32)


def dense(blocks):
    n, t, w = blocks.shape
    return blocks.astype(F32).reshape(n * t, w).astype(BF16)


def gelu_parts(hidden):
    cdf = 0.5 * (1.0 + lax.erf(hidden / math.sqrt(2.0)))
    pdf = jnp.exp(-0.5 * hidden * hidden) / math.sqrt(2.0 * math.pi)
    return (cdf, pdf)


def stack(blocks):
    return jnp.concatenate([block.astype(F32) for block in blocks], axis=0).astype(BF16)


def kernel(
    x_hbm, dy_hbm, wu_hbm, wd_hbm,
    xd_hbm, dyd_hbm, hgd_hbm, act_hbm, input_grad,
    act, xdt, wu, wu_sib, wd, wd_sib,
    xg, xd, dyd, hgd, dyb, sa, ra, ah1, ahs, ar2, sb, rb, eg, actb, hgb, sg, sgf, gh1, ghs, gr2, igs,
    local_sem, ss, rs, bss, brs, ess, ers, ass, ars,
):
    r, c = lax.axis_index("row"), lax.axis_index("col")
    z, k = r // 2, r % 2
    other = 1 - k
    sign = 1 - 2 * k
    px, py = c // 4, c % 4

    def wrap(v):
        return lax.rem(v + NZ, NZ)

    def zdev(d):
        return {"row": wrap(z + d) * 2 + k, "col": c}

    def pcol(dx, dy):
        return lax.rem(px + dx, 4) * 4 + lax.rem(py + dy, 4)

    def pdev(dx, dy):
        return {"row": r, "col": pcol(dx, dy)}

    sib = {"row": z * 2 + other, "col": c}
    copies = []

    def send(src, dst, dev):
        n = len(copies)
        copy = pltpu.make_async_remote_copy(
            src_ref=src, dst_ref=dst, send_sem=ss.at[n], recv_sem=rs.at[n],
            device_id=dev, device_id_type=MESH,
        )
        copy.start()
        copies.append(copy)
        return copy

    maybe = []

    def send_column(src, dst, col, sends, n, recvs):
        there = pltpu.make_async_remote_copy(
            src_ref=src, dst_ref=dst.at[c], send_sem=sends.at[n], recv_sem=recvs.at[c],
            device_id={"row": r, "col": col}, device_id_type=MESH,
        )
        here = pltpu.make_async_copy(src, dst.at[c], recvs.at[c])
        pl.when(col != c)(there.start)
        pl.when(col == c)(here.start)
        maybe.append((col != c, there))

    def wait_columns(dst, sends, recvs):
        for j in range(NP):
            pltpu.make_async_remote_copy(
                src_ref=dst.at[j], dst_ref=dst.at[j], send_sem=sends.at[j], recv_sem=recvs.at[j],
                device_id=sib, device_id_type=MESH,
            ).wait_recv()

    def gather_start(buf):
        return {-d: send(buf.at[z], buf.at[z], zdev(d)) for d in (6, -6, 3, -3, 1, -1)}

    def gather_relay(buf, got, d):
        got[d].wait_recv()
        block = wrap(z + d)
        for e in (1, -1):
            got[d - e] = send(buf.at[block], buf.at[block], zdev(e))

    def gather_far(buf, got):
        block = wrap(z - 6 * sign)
        got[8] = send(buf.at[block], buf.at[block], zdev(2 * sign))

    def reduce_start(buf, h1, ds=(8, -5, 7, -7, 5, -2, 4, -4, 2, 1, -1)):
        out = {}
        for d in ds:
            if d in SLOTS:
                slot, e = SLOTS[d]
                out[slot] = send(buf.at[wrap(z + d)], h1.at[slot], zdev(-2 * sign if d == 8 else e))
        return out

    def reduce_hub(buf, h1, hs, r2, first):
        first[10].wait_recv()
        far = h1[10].astype(F32)
        second = []
        for slot, d in ((1, -6), (3, 6), (0, -3), (2, 3)):
            first[slot].wait_recv()
            first[5 + slot].wait_recv()
            total = buf[wrap(z + d)].astype(F32) + h1[slot].astype(F32) + h1[5 + slot].astype(F32)
            if d == -6:
                total = total + jnp.where(k == 0, far, 0.0)
            if d == 6:
                total = total + jnp.where(k == 1, far, 0.0)
            hs[slot] = total.astype(BF16)
            second.append(send(hs.at[slot], r2.at[slot], zdev(d)))
        return second

    def reduce_end(buf, h1, r2, first, second):
        first[4].wait_recv()
        first[9].wait_recv()
        total = buf[z].astype(F32) + h1[4].astype(F32) + h1[9].astype(F32)
        for copy in second:
            copy.wait_recv()
        for slot in range(4):
            total = total + r2[slot].astype(F32)
        return total

    mine = pl.multiple_of(k * W, 16)
    theirs = pl.multiple_of(other * W, 16)
    load_x = pltpu.make_async_copy(x_hbm, xg.at[k, z], local_sem.at[0])
    load_dy = pltpu.make_async_copy(dy_hbm, dyb.at[k, c], local_sem.at[1])
    load_wd = pltpu.make_async_copy(wd_hbm.at[pl.ds(mine, W)], wd, local_sem.at[2])
    load_wu = pltpu.make_async_copy(wu_hbm, wu, local_sem.at[3])
    load_x.start()
    load_dy.start()
    load_wd.start()
    load_wu.start()

    barrier = pltpu.get_barrier_semaphore()
    partners = [zdev(d) for d in (6, -6)] + [pdev(*o) for o in PLANE] + [zdev(d) for d in (3, -3, 2, -2, 1, -1)] + [sib]
    for dev in partners:
        pl.semaphore_signal(barrier, inc=1, device_id=dev, device_id_type=MESH)
    load_x.wait()
    load_dy.wait()
    pl.semaphore_wait(barrier, len(partners))

    x_got = gather_start(xg.at[k])
    dy_copies = {o: send(dyb.at[k, c], dyb.at[k, c], pdev(*o)) for o in PLANE}
    to_sib = {0: [send(dyb.at[k, c], dyb.at[k, c], sib)], 1: [], 2: [], 3: []}
    x_sib = {0: send(xg.at[k, z], xg.at[k, z], sib)}
    wd_copy = send(wd_hbm.at[pl.ds(theirs, W)], wd_sib, sib)

    a_copies = {}

    def forward(dx):
        for dy in NEAR_FIRST:
            if (dx, dy) != (0, 0):
                dy_copies[dx, dy].wait_recv()
                block = pcol(4 - dx, 4 - dy)
                to_sib[dx].append(send(dyb.at[k, block], dyb.at[k, block], sib))

    def act_part(dx):
        for copy in to_sib[dx]:
            copy.wait_recv()
        g = lax.rem(px + 4 - dx, 4)
        own = dense(dyb[k, pl.ds(4 * g, 4)])
        dyd[pl.ds(pl.multiple_of(g * 96, 96), 96), :] = own
        part = dot_nt(own, wd[...]) + dot_nt(dense(dyb[other, pl.ds(4 * g, 4)]), wd_sib[...])
        for i in range(4):
            sa[4 * g + i] = part[TB * i : TB * (i + 1)].astype(BF16)
        for dy in FAR_FIRST:
            if (dx, dy) != (0, 0):
                to = (4 - dx) % 4, dy
                a_copies[to] = send(sa.at[pcol(*to)], ra.at[c], pdev(*to))


    def x_forward(*ds):
        for d in ds:
            if d not in (3, -3, 6, -6):
                x_got[d].wait_recv()
            block = wrap(z + d)
            x_sib[d] = send(xg.at[k, block], xg.at[k, block], sib)

    def hidden_part(n):
        for d in ARRIVAL[n]:
            x_sib[d].wait_recv()
        blocks = [wrap(z + d) for d in ARRIVAL[n]]
        own = stack([xg[core, block] for block in blocks for core in range(2)])
        xd[96 * n : 96 * n + 96, :] = own
        part = dot(own, wu[...])
        for i, block in enumerate(blocks):
            sb[block] = part[TB * i : TB * (i + 1)].astype(BF16)
        for i, block in enumerate(blocks):
            send_column(sb.at[block], rb, block, bss, 4 * n + i, brs)

    forward(0)
    x_forward(1, -1)
    gather_relay(xg.at[k], x_got, 3)
    gather_relay(xg.at[k], x_got, -3)
    forward(1)
    load_wd.wait()
    wd_copy.wait_recv()
    wu_copy = send(wu_hbm.at[pl.ds(theirs, W)], wu_sib, sib)
    act_part(0)
    forward(3)
    act_part(1)
    x_forward(3, -3)
    forward(2)
    gather_relay(xg.at[k], x_got, 6)
    gather_relay(xg.at[k], x_got, -6)
    gather_far(xg.at[k], x_got)
    act_part(3)
    act_part(2)
    ra[c] = sa[c]
    x_forward(2, -2, 4, -4, 6, -6)
    load_wu.wait()
    hidden_part(0)
    hidden_part(1)
    x_forward(5, -5, 7, -7, 8)
    hidden_part(2)
    hidden_part(3)

    a_first = {}
    for d, (slot, e) in SLOTS.items():
        a_first[slot] = pltpu.make_async_remote_copy(
            src_ref=ra.at[wrap(z + d)], dst_ref=ah1.at[slot], send_sem=ass.at[slot], recv_sem=ars.at[slot],
            device_id=zdev(-2 * sign if d == 8 else e), device_id_type=MESH,
        )

    def pass_on(block):
        for d, (slot, _) in SLOTS.items():
            pl.when(block == wrap(z + d))(a_first[slot].start)

    pass_on(c)
    for dx, dy in reversed(PLANE):
        a_copies[dx, dy].wait_recv()
        pass_on(pcol(4 - dx, 4 - dy))
    a_second = reduce_hub(ra, ah1, ahs, ar2, a_first)

    wait_columns(rb, bss, brs)
    hidden = jnp.zeros((TB, W), F32)
    for i in range(NP):
        hidden = hidden + rb[i].astype(F32)
    cdf, pdf = gelu_parts(hidden)
    eg[z] = (hidden * cdf).astype(BF16)
    slope = cdf + hidden * pdf

    act_grad = reduce_end(ra, ah1, ar2, a_first, a_second)
    hgb[k, c] = (act_grad * slope).astype(BF16)
    f_copies = {o: send(hgb.at[k, c], hgb.at[k, c], pdev(*o)) for o in PLANE}
    f_sib = [send(hgb.at[k, c], hgb.at[k, c], sib)]
    e_got = gather_start(eg)

    def e_send(*ds):
        for d in ds:
            if d not in (0, 3, -3, 6, -6):
                e_got[d].wait_recv()
            block = wrap(z + d)
            send_column(eg.at[block], actb.at[k], block, ess, d + 7, ers)

    def f_forward(offsets):
        for dx, dy in offsets:
            f_copies[dx, dy].wait_recv()
            block = pcol(4 - dx, 4 - dy)
            f_sib.append(send(hgb.at[k, block], hgb.at[k, block], sib))

    f_forward(reversed(PLANE))
    gather_relay(eg, e_got, 3)
    gather_relay(eg, e_got, -3)
    wu_copy.wait_recv()
    for copy in f_sib:
        copy.wait_recv()
    g_first = {}
    for n in (3, 2, 1, 0):
        blocks = [wrap(z + d) for d in ARRIVAL[n]]
        own = stack([hgb[k, block] for block in blocks])
        hgd[96 * n : 96 * n + 96, :] = own
        part = dot_nt(own, wu[pl.ds(mine, W), :]) + dot_nt(
            stack([hgb[other, block] for block in blocks]), wu_sib[...]
        )
        for i, block in enumerate(blocks):
            sgf[block] = part[TB * i : TB * (i + 1)]
            sg[block] = part[TB * i : TB * (i + 1)].astype(BF16)
        g_first |= reduce_start(sg, gh1, ARRIVAL[n])
        if n == 3:
            gather_relay(eg, e_got, 6)
            gather_relay(eg, e_got, -6)
            gather_far(eg, e_got)
        if n == 2:
            e_send(0, 3, -3, 6, -6, 1, -1)
    e_send(2, -2, 4, -4)

    g_second = reduce_hub(sgf, gh1, ghs, gr2, g_first)
    e_send(5, -5, 7, -7, 8)
    xdt[...] = xd[...].T
    flush = [pltpu.make_async_copy(xdt, xd_hbm, local_sem.at[4])]
    flush.append(pltpu.make_async_copy(hgd, hgd_hbm, local_sem.at[5]))
    flush.append(pltpu.make_async_copy(dyd, dyd_hbm, local_sem.at[6]))
    for copy in flush:
        copy.start()
    wait_columns(actb.at[k], ess, ers)
    e_sib = send(actb.at[k], actb.at[k], sib)
    act[pl.ds(mine, W), :] = dense(actb[k]).T
    e_sib.wait_recv()
    act[pl.ds(theirs, W), :] = dense(actb[other]).T
    flush.append(pltpu.make_async_copy(act, act_hbm, local_sem.at[7]))
    flush[3].start()

    total = reduce_end(sgf, gh1, gr2, g_first, g_second).astype(BF16)
    i = lax.broadcasted_iota(jnp.int32, (16, TB), 0)
    j = lax.broadcasted_iota(jnp.int32, (16, TB), 1)
    igs[k] = dot(jnp.where(j == i + TD * other, 1.0, 0.0).astype(BF16), total).astype(BF16)
    ig_sib = send(igs.at[k], igs.at[k], sib)
    kept = dot(jnp.where(j == i + TD * k, 1.0, 0.0).astype(BF16), total)
    ig_sib.wait_recv()
    came = igs[other].astype(F32)
    halves = [jnp.where(k == 0, kept, came), jnp.where(k == 0, came, kept)]
    input_grad[...] = jnp.concatenate(halves, axis=1)[:TD].astype(BF16)
    for copy in flush:
        copy.wait()
    for copy in [*copies, *a_first.values()]:
        copy.wait_send()
    for sent, there in maybe:
        pl.when(sent)(there.wait_send)


def products(
    xd_hbm, dyd_hbm, hgd_hbm, act_hbm, ig_hbm, ig_out, up_hbm, down_hbm,
    xd, dyd, hgd, act, ig, up, down, load_sems, sems,
):
    pairs = (
        (ig_hbm, ig), (hgd_hbm, hgd), (xd_hbm.at[0:512], xd.at[0:512]), (xd_hbm.at[512:D2], xd.at[512:D2]),
        (dyd_hbm, dyd), (act_hbm.at[0:W], act.at[0:W]), (act_hbm.at[W:D2], act.at[W:D2]),
    )
    loads = [pltpu.make_async_copy(a, b, load_sems.at[n]) for n, (a, b) in enumerate(pairs)]
    for load in loads:
        load.start()
    copies = []

    def write(src, dst):
        copies.append(pltpu.make_async_copy(src, dst, sems.at[len(copies)]))
        copies[-1].start()

    loads[0].wait()
    write(ig, ig_out)
    loads[1].wait()
    for n, (low, high) in enumerate(((0, 512), (512, D2))):
        loads[2 + n].wait()
        up[low:high, :] = dot(xd[low:high, :], hgd[...])
        write(up.at[low:high], up_hbm.at[low:high])
    loads[4].wait()
    loads[5].wait()
    for low, high in ((0, W), (W, 768), (768, D2)):
        if low == W:
            loads[6].wait()
        down[low:high, :] = dot(act[low:high, :], dyd[...])
        write(down.at[low:high], down_hbm.at[low:high])
    for copy in copies:
        copy.wait()


def shards(inputs, out_grad, w_up, w_down):
    vmem = pl.BlockSpec(memory_space=pltpu.VMEM)
    hbm = pl.BlockSpec(memory_space=pltpu.HBM)

    def blocks(*lead):
        return pltpu.VMEM((*lead, TB, W), BF16)

    gathered = pl.pallas_call(
        kernel,
        name="feed_forward_backward",
        out_shape=[
            jax.ShapeDtypeStruct((D2, TOKENS), BF16),
            jax.ShapeDtypeStruct((TOKENS, W), BF16),
            jax.ShapeDtypeStruct((TOKENS, W), BF16),
            jax.ShapeDtypeStruct((D2, TOKENS), BF16),
            jax.ShapeDtypeStruct((TD, D2), BF16),
        ],
        in_specs=[hbm] * 4,
        out_specs=[hbm] * 4 + [vmem],
        scratch_shapes=[
            pltpu.VMEM((D2, TOKENS), BF16), pltpu.VMEM((D2, TOKENS), BF16), pltpu.VMEM((D2, W), BF16), pltpu.VMEM((W, W), BF16), pltpu.VMEM((W, W), BF16), pltpu.VMEM((W, W), BF16),
            pltpu.VMEM((2, NZ, TD, D2), BF16), pltpu.VMEM((TOKENS, D2), BF16),
            pltpu.VMEM((TOKENS, W), BF16), pltpu.VMEM((TOKENS, W), BF16), blocks(2, NP),
            blocks(NP), blocks(NP), blocks(11), blocks(4), blocks(4),
            blocks(NP), blocks(NP), blocks(NZ), blocks(2, NP), blocks(2, NP),
            blocks(NZ), pltpu.VMEM((NZ, TB, W), F32), blocks(11), blocks(4), blocks(4),
            pltpu.VMEM((2, 16, W), BF16),
            pltpu.SemaphoreType.DMA((8,)), pltpu.SemaphoreType.DMA((COPIES,)), pltpu.SemaphoreType.DMA((COPIES,)),
            pltpu.SemaphoreType.DMA((NP,)), pltpu.SemaphoreType.DMA((NP,)),
            pltpu.SemaphoreType.DMA((NP,)), pltpu.SemaphoreType.DMA((NP,)),
            pltpu.SemaphoreType.DMA((11,)), pltpu.SemaphoreType.DMA((11,)),
        ],
        compiler_params=pltpu.CompilerParams(
            collective_id=0, has_side_effects=True, vmem_limit_bytes=60 * 2**20
        ),
    )(inputs, out_grad, w_up, w_down)
    return pl.pallas_call(
        products,
        name="weight_gradients",
        out_shape=[
            jax.ShapeDtypeStruct((TD, D2), BF16),
            jax.ShapeDtypeStruct((D2, W), F32),
            jax.ShapeDtypeStruct((D2, W), F32),
        ],
        in_specs=[hbm] * 5,
        out_specs=[hbm] * 3,
        scratch_shapes=[
            pltpu.VMEM((D2, TOKENS), BF16), pltpu.VMEM((TOKENS, W), BF16), pltpu.VMEM((TOKENS, W), BF16),
            pltpu.VMEM((D2, TOKENS), BF16), pltpu.VMEM((TD, D2), BF16),
            pltpu.VMEM((D2, W), F32), pltpu.VMEM((D2, W), F32),
            pltpu.SemaphoreType.DMA((7,)), pltpu.SemaphoreType.DMA((6,)),
        ],
        compiler_params=pltpu.CompilerParams(vmem_limit_bytes=60 * 2**20),
    )(*gathered)


def solution(mesh):
    return jax.shard_map(
        shards,
        mesh=mesh,
        in_specs=(P("row", "col"), P("col", "row"), P("col", "row"), P("col", "row")),
        out_specs=(P("row", "col"), P("col", "row"), P("col", "row")),
        check_vma=False,
    )
```
